32 devices in a mesh: row: 4 (over y, x), col: 8 (over z, core).
Axes of the slice: x: 2, y: 2, z: 4, core: 2. Of those that a mesh axis runs over, the one named last changes fastest.
Arguments:
- front_orig: float32 [6144, 6144], P('row', 'col')
- pivot_shift: float32 [6144], replicated, may hold values from 4.5 to 9
- child_update: float32 [8192, 4096], P('row', 'col'), may hold values from -0.0625 to 0.0625
- child_map: int32 [2, 16], replicated, may hold values from 0 to 23, as said below
Outputs:
- front_out: float32 [6144, 6144], P('row', 'col')
The draws below stay inside these ranges and needn't reach their ends.
Inputs may be any that keep to these rules, and one draw needn't show every extreme that they name: Child h's block b (rows and columns alike) goes to parent block child_map[h, b]; child_map[h, b] % 8 == b % 8; the two child blocks b and b + 8 (b < 8) take two different ones of the parent blocks b, b + 8, b + 16, the smaller child block to the smaller parent block.
All inputs are finite; a program needn't handle non-finite values.
Results may differ from the reference program's by a relative error of at most 0.0001.
Values sent between devices are 32-bit elements; how exact they have to be, the bound alone decides.
A program may use at most 128 MiB of HBM per device.

```python
import jax
import jax.numpy as jnp
from jax import lax

BS = 256
PANELS = 6
CB = 16
F = 6144
C = 4096
N_ROW = 4
N_COL = 8


def draw_front_orig(key, part):
    spread = jnp.float32(F) ** (-0.5)
    values = jnp.abs(jnp.clip(jax.random.normal(key, (F, F), jnp.float32), -6.0, 6.0)) * spread
    return values.astype(jnp.float32)


def draw_child_map(key, part):
    residues = CB // 2
    skipped = jax.random.randint(key, (2, residues), 0, 3)
    opening = 1 + jax.random.randint(jax.random.fold_in(key, 11), (), 0, 2)
    closing = jax.random.randint(jax.random.fold_in(key, 12), (), 0, 2)
    skipped = skipped.at[0, 0].set(opening).at[0, residues - 1].set(closing)
    lower_slot = jnp.where(skipped == 0, 1, 0)
    upper_slot = jnp.where(skipped == 2, 1, 2)
    residue = jnp.arange(residues, dtype=jnp.int32)[None, :]
    first_half = residue + residues * lower_slot
    second_half = residue + residues * upper_slot
    return jnp.concatenate([first_half, second_half], axis=1).astype(jnp.int32)


def levels(own_key, dims, shards, smallest, largest):
    def one(axis_at, shards_of):
        draws = jax.random.uniform(jax.random.fold_in(jax.random.fold_in(own_key, 6), axis_at), (shards_of,), jnp.float32, smallest / len(shards), largest / len(shards))
        return jnp.repeat(jnp.exp(draws), dims[axis_at] // shards_of).reshape((-1,) + (1,) * (len(dims) - axis_at - 1))

    gain = one(*shards[0])
    for cut in shards[1:]:
        gain = gain * one(*cut)
    return gain


def scatter_about(own_key, extent, scale, reach, pieces=(), kind=jnp.bfloat16):
    values = jax.random.normal(own_key, extent, jnp.float32) * scale
    if len(pieces) > 0:
        values = levels(own_key, extent, pieces, -0.22, 0.18) * values
    return jnp.clip(values, min=-reach, max=reach).astype(kind)


def setup_inputs(seed: int = 0) -> dict:
    streams_of = jax.random.split(jax.random.key(seed), 5)
    front_orig = draw_front_orig(jax.random.fold_in(streams_of[4], 71), 0)
    pivot_shift = jnp.clip(jax.random.uniform(streams_of[1], (F,), jnp.float32, 4.5, 9.0), 4.5, 9.0)
    child_update = scatter_about(streams_of[2], (2 * C, C), (2 * C) ** -0.5, 0.0625, ((0, 4), (1, 8)), jnp.float32)
    child_map = draw_child_map(jax.random.fold_in(streams_of[4], 71), 0)
    return {"front_orig": front_orig, "pivot_shift": pivot_shift, "child_update": child_update, "child_map": child_map}


def natural_order(stored, rows_dev, cols_dev):
    total_rows, total_cols = stored.shape
    row_tiles = total_rows // BS // rows_dev
    col_tiles = total_cols // BS // cols_dev
    shaped = stored.reshape(rows_dev, row_tiles, BS, cols_dev, col_tiles, BS)
    return shaped.transpose(1, 0, 2, 4, 3, 5).reshape(total_rows, total_cols)

def storage_order(natural, rows_dev, cols_dev):
    total_rows, total_cols = natural.shape
    row_tiles = total_rows // BS // rows_dev
    col_tiles = total_cols // BS // cols_dev
    shaped = natural.reshape(row_tiles, rows_dev, BS, col_tiles, cols_dev, BS)
    return shaped.transpose(1, 0, 2, 4, 3, 5).reshape(total_rows, total_cols)

def symmetric_block(pivot_block):
    return jnp.tril(pivot_block) + jnp.tril(pivot_block, -1).T

def reference(front_orig, pivot_shift, child_update, child_map):
    front_now = natural_order(front_orig, N_ROW, N_COL)
    diagonal = jnp.arange(F, dtype=jnp.int32)
    front_now = front_now.at[diagonal, diagonal].add(pivot_shift)
    offsets = jnp.arange(BS, dtype=jnp.int32)
    for child_id in range(2):
        update = natural_order(child_update[child_id * C:(child_id + 1) * C], N_ROW // 2, N_COL)
        placement = (child_map[child_id].astype(jnp.int32)[:, None] * BS + offsets[None, :]).reshape(-1)
        front_now = front_now.at[placement[:, None], placement[None, :]].add(update)
    for panel_id in range(PANELS):
        first_row = panel_id * BS
        finish = first_row + BS
        factor = jnp.linalg.cholesky(symmetric_block(front_now[first_row:finish, first_row:finish]))
        below = lax.linalg.triangular_solve(factor, front_now[finish:, first_row:finish], left_side=False, lower=True, transpose_a=True)
        front_now = front_now.at[first_row:finish, first_row:finish].set(factor)
        front_now = front_now.at[finish:, first_row:finish].set(below)
        product = jnp.dot(below, below.T, precision=lax.Precision.HIGHEST)
        front_now = front_now.at[finish:, finish:].add(-product)
    return storage_order(front_now, N_ROW, N_COL)
```

```python
import functools

import jax
import jax.numpy as jnp
from jax import lax
from jax.experimental import pallas as pl
from jax.experimental.pallas import tpu as pltpu
from jax.sharding import PartitionSpec as P

BS = 256
PANELS = 6
STRIP = 32
VMEM_BYTES = 52 * 1024 * 1024
NT = (((1,), (1,)), ((), ()))
TN = (((0,), (0,)), ((), ()))


def split(x):
    high = x.astype(jnp.bfloat16)
    low = (x - high.astype(jnp.float32)).astype(jnp.bfloat16)
    return high, low


def mul_nt(a, b):
    a_high, a_low = a
    b_high, b_low = b
    dot = functools.partial(lax.dot_general, dimension_numbers=NT, preferred_element_type=jnp.float32)
    return dot(a_high, b_high) + (dot(a_high, b_low) + dot(a_low, b_high))


def params():
    return pltpu.CompilerParams(vmem_limit_bytes=VMEM_BYTES)


def vmem():
    return pl.BlockSpec(memory_space=pltpu.VMEM)


def smem():
    return pl.BlockSpec(memory_space=pltpu.SMEM)


def column_kernel(info_ref, front_ref, shift_ref, stay_ref, come_ref, out_ref):
    p = pl.program_id(0)
    rows = lax.broadcasted_iota(jnp.int32, (BS, BS), 0)
    cols = lax.broadcasted_iota(jnp.int32, (BS, BS), 1)
    on_diag = (rows == cols) & (info_ref[4, p] == info_ref[5, 0])
    total = front_ref[...] + jnp.where(on_diag, shift_ref[...], 0.0)
    total += jnp.where((info_ref[2, p] > 0) & (info_ref[6, 0] == 0), stay_ref[...], 0.0)
    total += jnp.where((info_ref[3, p] > 0) & (info_ref[7, 0] == 0), come_ref[0], 0.0)
    out_ref[...] = total


def panel_column(info, front, shift, child, come):
    local_rows = front.shape[0] // BS
    grid_spec = pltpu.PrefetchScalarGridSpec(
        num_scalar_prefetch=1,
        grid=(local_rows,),
        in_specs=[
            pl.BlockSpec((BS, BS), lambda p, s: (p, 0)),
            pl.BlockSpec((1, BS), lambda p, s: (0, s[4, p])),
            pl.BlockSpec((BS, BS), lambda p, s: (s[0, p], 0)),
            pl.BlockSpec((1, BS, BS), lambda p, s: (s[1, p], 0, 0)),
        ],
        out_specs=pl.BlockSpec((BS, BS), lambda p, s: (p, 0)),
    )
    return pl.pallas_call(
        column_kernel,
        grid_spec=grid_spec,
        out_shape=jax.ShapeDtypeStruct((local_rows * BS, BS), jnp.float32),
        compiler_params=params(),
    )(info, front, shift, child, come)


def cholesky_steps(work):
    row = lax.broadcasted_iota(jnp.int32, (STRIP, 1), 0)
    wide_row = lax.broadcasted_iota(jnp.int32, (STRIP, 2 * BS), 0)
    wide_col = lax.broadcasted_iota(jnp.int32, (STRIP, 2 * BS), 1)
    for strip in range(BS // STRIP):
        first = strip * STRIP
        panel = work[first : first + STRIP, :]
        for j in range(STRIP):
            column = panel[:, first + j : first + j + 1]
            factor = jnp.where(row > j, column / column[j : j + 1], 0.0)
            panel = panel - factor * panel[j : j + 1, :]
        diag = jnp.sum(jnp.where(wide_col == wide_row + first, panel, 0.0), axis=1, keepdims=True)
        scale = 1.0 / jnp.sqrt(diag)
        panel = jnp.where(wide_col >= wide_row + first, panel * scale, 0.0)
        work[first : first + STRIP, :] = panel
        after = first + STRIP
        if after < BS:
            step = lax.dot_general(
                panel[:, :BS],
                panel,
                TN,
                precision=lax.Precision.HIGHEST,
                preferred_element_type=jnp.float32,
            )
            work[after:, :] = work[after:, :] - step[after:, :]


def lead_kernel(where_block, side_ref, mine_ref, other_ref, low_ref, inv_ref, up_ref, work):
    first = side_ref[0] == 0
    for j in range(PANELS):
        for i in range(PANELS):
            dest = low_ref.at[j, i * BS : (i + 1) * BS, :]
            if i < j:
                dest[...] = jnp.zeros((BS, BS), jnp.float32)
            else:
                owner, half, place = where_block[(i, j)]
                mine = mine_ref[owner, place]
                other = other_ref[owner, place]
                dest[...] = jnp.where(first == (half == 0), mine, other)
    rows = lax.broadcasted_iota(jnp.int32, (BS, BS), 0)
    cols = lax.broadcasted_iota(jnp.int32, (BS, BS), 1)

    def step(k, carry):
        start = pl.multiple_of(k * BS, BS)
        pivot = low_ref[k, pl.ds(start, BS), :]
        work[:, :BS] = jnp.where(rows >= cols, pivot, pivot.T)
        work[:, BS:] = jnp.where(rows == cols, 1.0, 0.0)
        cholesky_steps(work)
        up_ref[k] = work[:, :BS]
        inverse = work[:, BS:]
        inv_ref[k] = inverse
        inverse = split(inverse)

        def solve(i, carry):
            at = pl.ds(pl.multiple_of(i * BS, BS), BS)
            low_ref[k, at, :] = mul_nt(split(low_ref[k, at, :]), inverse)
            return carry

        lax.fori_loop(k + 1, PANELS, solve, 0)

        def update(j, carry):
            at_j = pl.ds(pl.multiple_of(j * BS, BS), BS)
            right = split(low_ref[k, at_j, :])

            def one(i, carry):
                at = pl.ds(pl.multiple_of(i * BS, BS), BS)
                low_ref[j, at, :] = low_ref[j, at, :] - mul_nt(split(low_ref[k, at, :]), right)
                return carry

            return lax.fori_loop(j, PANELS, one, carry)

        lax.fori_loop(k + 1, PANELS, update, 0)
        return carry

    lax.fori_loop(0, PANELS, step, 0)


def factor_lead(where_block, side, mine, other):
    return pl.pallas_call(
        functools.partial(lead_kernel, where_block),
        in_specs=[smem(), vmem(), vmem()],
        out_specs=[vmem(), vmem(), vmem()],
        out_shape=[
            jax.ShapeDtypeStruct((PANELS, PANELS * BS, BS), jnp.float32),
            jax.ShapeDtypeStruct((PANELS, BS, BS), jnp.float32),
            jax.ShapeDtypeStruct((PANELS, BS, BS), jnp.float32),
        ],
        scratch_shapes=[pltpu.VMEM((BS, 2 * BS), jnp.float32)],
        compiler_params=params(),
    )(side, mine, other)


def solve_kernel(blocks, ids_ref, rows_ref, low_ref, inv_ref, out_ref):
    step = pl.program_id(0)
    done = []
    for k in range(PANELS):
        total = rows_ref[k]
        for j in range(k):
            total = total - mul_nt(done[j], split(low_ref[j, k * BS : (k + 1) * BS, :]))
        solved = mul_nt(split(total), split(inv_ref[k]))
        parts = []
        for b in range(blocks):
            live = ids_ref[step * blocks + b] > k
            parts.append(jnp.where(live, solved[b * BS : (b + 1) * BS], 0.0))
        solved = jnp.concatenate(parts, axis=0) if blocks > 1 else parts[0]
        out_ref[k] = solved
        done.append(split(solved))


def solve_rows(ids, rows, low, inv, blocks):
    count = rows.shape[1] // (blocks * BS)
    return pl.pallas_call(
        functools.partial(solve_kernel, blocks),
        grid=(count,),
        in_specs=[
            smem(),
            pl.BlockSpec((PANELS, blocks * BS, BS), lambda i: (0, i, 0)),
            vmem(),
            vmem(),
        ],
        out_specs=pl.BlockSpec((PANELS, blocks * BS, BS), lambda i: (0, i, 0)),
        out_shape=jax.ShapeDtypeStruct((PANELS, rows.shape[1], BS), jnp.float32),
        compiler_params=params(),
    )(ids, rows, low, inv)


def trail_kernel(
    head, local_cols, info_ref, front_ref, shift_ref, stay_ref, come0_ref, come1_ref,
    lead_ref, rest_ref, across_ref, factor_ref, out_ref, high_ref, low_ref,
):
    p = pl.program_id(0)

    @pl.when(p == 0)
    def _():
        for k in range(PANELS):
            high, low = split(across_ref[k])
            high_ref[k] = high
            low_ref[k] = low

    in_head = p < head
    total = jnp.zeros((BS, local_cols * BS), jnp.float32)
    for k in range(PANELS):
        left = split(jnp.where(in_head, lead_ref[k], rest_ref[k]))
        total = total + mul_nt(left, (high_ref[k], low_ref[k]))
    rows = lax.broadcasted_iota(jnp.int32, (BS, BS), 0)
    cols = lax.broadcasted_iota(jnp.int32, (BS, BS), 1)
    row_id = info_ref[4, p]
    panel = info_ref[8, 0]
    stays = info_ref[2, p] > 0
    comes = info_ref[3, p] > 0
    for s in range(local_cols):
        at = slice(s * BS, (s + 1) * BS)
        on_diag = (rows == cols) & (row_id == info_ref[5, s])
        block = front_ref[:, at] + jnp.where(on_diag, shift_ref[...], 0.0)
        for u, come_ref in enumerate((come0_ref, come1_ref)):
            piece = stay_ref[:, u * BS : (u + 1) * BS]
            block += jnp.where(stays & (info_ref[6, u] == s), piece, 0.0)
            block += jnp.where(comes & (info_ref[7, u] == s), come_ref[0], 0.0)
        block = block - total[:, at]
        if s == 0:
            own = jnp.where(in_head, lead_ref[panel], rest_ref[panel])
            in_panel = info_ref[9, 0] > 0
            block = jnp.where(in_panel & (row_id > panel), own, block)
            block = jnp.where(in_panel & (row_id == panel), factor_ref[...], block)
        out_ref[:, at] = block


def trail(info, front, shift, child, come0, come1, lead, rest, across, factor):
    local_rows = front.shape[0] // BS
    local_cols = front.shape[1] // BS
    head = lead.shape[1] // BS
    grid_spec = pltpu.PrefetchScalarGridSpec(
        num_scalar_prefetch=1,
        grid=(local_rows,),
        in_specs=[
            pl.BlockSpec((BS, local_cols * BS), lambda p, s: (p, 0)),
            pl.BlockSpec((1, BS), lambda p, s: (0, s[4, p])),
            pl.BlockSpec((BS, child.shape[1]), lambda p, s: (s[0, p], 0)),
            pl.BlockSpec((1, BS, BS), lambda p, s: (s[1, p], 0, 0)),
            pl.BlockSpec((1, BS, BS), lambda p, s: (s[1, p], 0, 0)),
            pl.BlockSpec((PANELS, BS, BS), lambda p, s: (0, jnp.minimum(p, head - 1), 0)),
            pl.BlockSpec((PANELS, BS, BS), lambda p, s: (0, jnp.maximum(p - head, 0), 0)),
            pl.BlockSpec(across.shape, lambda p, s: (0, 0, 0)),
            pl.BlockSpec((BS, BS), lambda p, s: (0, 0)),
        ],
        out_specs=pl.BlockSpec((BS, local_cols * BS), lambda p, s: (p, 0)),
        scratch_shapes=[pltpu.VMEM(across.shape, jnp.bfloat16)] * 2,
    )
    return pl.pallas_call(
        functools.partial(trail_kernel, head, local_cols),
        grid_spec=grid_spec,
        out_shape=jax.ShapeDtypeStruct(front.shape, jnp.float32),
        compiler_params=params(),
    )(info, front, shift, child, come0, come1, lead, rest, across, factor)


def on_device(front_orig, pivot_shift, child_update, child_map):
    n_row = lax.axis_size("row")
    n_col = lax.axis_size("col")
    row_id = lax.axis_index("row")
    col_id = lax.axis_index("col")
    half_rows = n_row // 2
    local_rows = front_orig.shape[0] // BS
    local_cols = front_orig.shape[1] // BS
    pair_count = child_update.shape[0] // BS // 2
    child_cols = child_update.shape[1] // BS
    stride = n_col // n_row
    head = stride
    side = row_id // half_rows

    paired = child_update.reshape(pair_count, 2, BS, child_cols, BS)
    swap = [(i, i ^ half_rows) for i in range(n_row)]
    come = [
        lax.ppermute(
            lax.dynamic_index_in_dim(paired[:, :, :, u], 1 - side, axis=1, keepdims=False),
            "row",
            swap,
        )
        for u in range(child_cols)
    ]

    mine_map = child_map[side]
    other_map = child_map[1 - side]
    slots = jnp.arange(local_rows, dtype=jnp.int32)

    def rows_of(table):
        wanted = table.reshape(pair_count, n_row)
        wanted = lax.dynamic_index_in_dim(wanted, row_id, axis=1, keepdims=False) // n_row
        hit = wanted[None, :] == slots[:, None]
        q = jnp.sum(jnp.where(hit, jnp.arange(pair_count, dtype=jnp.int32)[None, :], 0), axis=1)
        return q, jnp.any(hit, axis=1).astype(jnp.int32)

    def cols_of(table):
        wanted = table.reshape(child_cols, n_col)
        return lax.dynamic_index_in_dim(wanted, col_id, axis=1, keepdims=False) // n_col

    def line(values):
        values = jnp.atleast_1d(values).astype(jnp.int32)
        return jnp.pad(values, (0, 8 - values.shape[0]))

    stay_q, stays = rows_of(mine_map)
    come_q, comes = rows_of(other_map)
    row_blocks = slots * n_row + row_id
    col_blocks = jnp.arange(local_cols, dtype=jnp.int32) * n_col + col_id
    info = jnp.stack(
        [
            line(2 * stay_q + side),
            line(come_q),
            line(stays),
            line(comes),
            line(row_blocks),
            line(col_blocks),
            line(cols_of(mine_map)),
            line(cols_of(other_map)),
            line(jnp.minimum(col_id, PANELS - 1)),
            line(col_id < PANELS),
        ]
    )
    shift = pivot_shift.reshape(1, -1)
    column = panel_column(info, front_orig, shift, child_update, come[0])

    lead_rows = lax.all_gather(column[: head * BS], "col", axis=0)[:PANELS]
    rest_rows = lax.all_gather(column[head * BS :], "col", axis=0)[:PANELS]

    lists = [
        [(i, j) for i in range(r, PANELS, n_row) for j in range(i + 1)] for r in range(n_row)
    ]
    length = max(len(blocks) for blocks in lists)
    length += length % 2
    width = length // 2
    where_block = {}
    table = []
    for r, blocks in enumerate(lists):
        entry = [j * head + (i // n_row) for i, j in blocks]
        table.append(entry + [0] * (length - len(entry)))
        for e, block in enumerate(blocks):
            where_block[block] = (r, e // width, e % width)
    table = jnp.array(table, jnp.int32).reshape(n_row, 2, width)
    parity = col_id % 2
    picks = table[row_id, parity]
    lead_tiles = lead_rows.reshape(PANELS * head, BS, BS)
    sent = jnp.stack(
        [lax.dynamic_index_in_dim(lead_tiles, picks[e], axis=0, keepdims=False) for e in range(width)]
    )
    mine = lax.all_gather(sent, "row", axis=0)
    other = lax.ppermute(mine, "col", [(i, i ^ 1) for i in range(n_col)])
    low, inv, up = factor_lead(where_block, parity.reshape(1), mine, other)

    pick = col_id // n_row
    source = col_id % n_row
    first = lax.dynamic_index_in_dim(
        lead_rows.reshape(PANELS, 1, head, BS, BS), pick, axis=2, keepdims=False
    )
    others = lax.dynamic_index_in_dim(
        rest_rows.reshape(PANELS, local_cols - 1, head, BS, BS), pick, axis=2, keepdims=False
    )
    across = jnp.concatenate([first, others], axis=1).reshape(PANELS, local_cols * BS, BS)
    across = jnp.where(row_id == source, across, 0.0)
    bit = half_rows
    held = [0]
    while bit:
        pairs = [
            (((c % n_row) ^ h) * n_col + c, ((c % n_row) ^ h ^ bit) * n_col + c)
            for c in range(n_col)
            for h in held
        ]
        across = across + lax.ppermute(across, ("row", "col"), pairs)
        held = held + [h ^ bit for h in held]
        bit //= 2

    lead = solve_rows(row_blocks[:head], lead_rows, low, inv, head)
    rest = solve_rows(row_blocks[head:], rest_rows, low, inv, head)
    across = solve_rows(col_blocks, across, low, inv, local_cols)
    factor = lax.dynamic_index_in_dim(
        up, jnp.minimum(col_id, PANELS - 1), axis=0, keepdims=False
    ).T
    return trail(
        info, front_orig, shift, child_update, come[0], come[1], lead, rest, across, factor
    )


def solution(mesh):
    in_specs = (P("row", "col"), P(), P("row", "col"), P())
    out_specs = P("row", "col")
    return jax.shard_map(
        on_device, mesh=mesh, in_specs=in_specs, out_specs=out_specs, check_vma=False
    )
```

```python
import functools

import jax
import jax.numpy as jnp
from jax import lax
from jax.experimental import pallas as pl
from jax.experimental.pallas import tpu as pltpu
from jax.sharding import PartitionSpec as P

BS = 256
PANELS = 6
STRIP = 32
GROUP = 2
VMEM_BYTES = 52 * 1024 * 1024
NT = (((1,), (1,)), ((), ()))
TN = (((0,), (0,)), ((), ()))


def split(x):
    high = x.astype(jnp.bfloat16)
    low = (x - high.astype(jnp.float32)).astype(jnp.bfloat16)
    return high, low


def mul_nt(a, b):
    a_high, a_low = a
    b_high, b_low = b
    dot = functools.partial(lax.dot_general, dimension_numbers=NT, preferred_element_type=jnp.float32)
    return dot(a_high, b_high) + (dot(a_high, b_low) + dot(a_low, b_high))


def params():
    return pltpu.CompilerParams(vmem_limit_bytes=VMEM_BYTES)


def vmem():
    return pl.BlockSpec(memory_space=pltpu.VMEM)


def smem():
    return pl.BlockSpec(memory_space=pltpu.SMEM)


def column_kernel(info_ref, front_ref, shift_ref, stay_ref, come_ref, out_ref):
    p = pl.program_id(0)
    rows = lax.broadcasted_iota(jnp.int32, (BS, BS), 0)
    cols = lax.broadcasted_iota(jnp.int32, (BS, BS), 1)
    on_diag = (rows == cols) & (info_ref[4, p] == info_ref[5, 0])
    total = front_ref[...] + jnp.where(on_diag, shift_ref[...], 0.0)
    total += jnp.where((info_ref[2, p] > 0) & (info_ref[6, 0] == 0), stay_ref[...], 0.0)
    total += jnp.where((info_ref[3, p] > 0) & (info_ref[7, 0] == 0), come_ref[0], 0.0)
    out_ref[...] = total


def panel_column(info, front, shift, child, come):
    local_rows = front.shape[0] // BS
    grid_spec = pltpu.PrefetchScalarGridSpec(
        num_scalar_prefetch=1,
        grid=(local_rows,),
        in_specs=[
            pl.BlockSpec((BS, BS), lambda p, s: (p, 0)),
            pl.BlockSpec((1, BS), lambda p, s: (0, s[4, p])),
            pl.BlockSpec((BS, BS), lambda p, s: (s[0, p], 0)),
            pl.BlockSpec((1, BS, BS), lambda p, s: (s[1, p], 0, 0)),
        ],
        out_specs=pl.BlockSpec((BS, BS), lambda p, s: (p, 0)),
    )
    return pl.pallas_call(
        column_kernel,
        grid_spec=grid_spec,
        out_shape=jax.ShapeDtypeStruct((local_rows * BS, BS), jnp.float32),
        compiler_params=params(),
    )(info, front, shift, child, come)


def cholesky_steps(work):
    row = lax.broadcasted_iota(jnp.int32, (STRIP, 1), 0)
    half = BS // 2
    for strip in range(BS // STRIP):
        first = strip * STRIP
        after = first + STRIP
        lo = first // half * half
        hi = BS + (after + half - 1) // half * half
        wide_row = lax.broadcasted_iota(jnp.int32, (STRIP, hi - lo), 0) + first
        wide_col = lax.broadcasted_iota(jnp.int32, (STRIP, hi - lo), 1) + lo
        panel = work[first:after, lo:hi]
        for j in range(STRIP):
            at = first - lo + j
            column = panel[:, at : at + 1]
            factor = jnp.where(row > j, column / column[j : j + 1], 0.0)
            panel = panel - factor * panel[j : j + 1, :]
        diag = jnp.sum(jnp.where(wide_col == wide_row, panel, 0.0), axis=1, keepdims=True)
        scale = 1.0 / jnp.sqrt(diag)
        panel = jnp.where(wide_col >= wide_row, panel * scale, 0.0)
        work[first:after, lo:hi] = panel
        if after < BS:
            step = lax.dot_general(
                panel[:, : BS - lo],
                panel,
                TN,
                precision=lax.Precision.HIGHEST,
                preferred_element_type=jnp.float32,
            )
            work[after:, lo:hi] = work[after:, lo:hi] - step[after - lo :, :]


def lead_kernel(where_block, side_ref, mine_ref, other_ref, low_ref, inv_ref, up_ref, work):
    first = side_ref[0] == 0
    for j in range(PANELS):
        for i in range(PANELS):
            dest = low_ref.at[j, i * BS : (i + 1) * BS, :]
            if i < j:
                dest[...] = jnp.zeros((BS, BS), jnp.float32)
            else:
                owner, half, place = where_block[(i, j)]
                mine = mine_ref[owner, place]
                other = other_ref[owner, place]
                dest[...] = jnp.where(first == (half == 0), mine, other)
    factor_panels(0, low_ref, inv_ref, up_ref, work)


def more_kernel(start, before_ref, low_ref, inv_ref, up_ref, work):
    low_ref[...] = before_ref[...]
    factor_panels(start, low_ref, inv_ref, up_ref, work)


def factor_panels(begin, low_ref, inv_ref, up_ref, work):
    rows = lax.broadcasted_iota(jnp.int32, (BS, BS), 0)
    cols = lax.broadcasted_iota(jnp.int32, (BS, BS), 1)

    def step(k, carry):
        start = pl.multiple_of(k * BS, BS)
        pivot = low_ref[k, pl.ds(start, BS), :]
        work[:, :BS] = jnp.where(rows >= cols, pivot, pivot.T)
        work[:, BS:] = jnp.where(rows == cols, 1.0, 0.0)
        cholesky_steps(work)
        up_ref[k - begin] = jnp.where(cols >= rows, work[:, :BS], 0.0)
        inverse = work[:, BS:]
        inv_ref[k - begin] = inverse
        inverse = split(inverse)

        def solve(i, carry):
            at = pl.ds(pl.multiple_of(i * BS, BS), BS)
            low_ref[k, at, :] = mul_nt(split(low_ref[k, at, :]), inverse)
            return carry

        lax.fori_loop(k + 1, PANELS, solve, 0)

        def update(j, carry):
            at_j = pl.ds(pl.multiple_of(j * BS, BS), BS)
            right = split(low_ref[k, at_j, :])

            def one(i, carry):
                at = pl.ds(pl.multiple_of(i * BS, BS), BS)
                low_ref[j, at, :] = low_ref[j, at, :] - mul_nt(split(low_ref[k, at, :]), right)
                return carry

            return lax.fori_loop(j, PANELS, one, carry)

        lax.fori_loop(k + 1, PANELS, update, 0)
        return carry

    lax.fori_loop(begin, begin + GROUP, step, 0)


def factor_group(kernel, operands, in_specs):
    return pl.pallas_call(
        kernel,
        in_specs=in_specs,
        out_specs=[vmem(), vmem(), vmem()],
        out_shape=[
            jax.ShapeDtypeStruct((PANELS, PANELS * BS, BS), jnp.float32),
            jax.ShapeDtypeStruct((GROUP, BS, BS), jnp.float32),
            jax.ShapeDtypeStruct((GROUP, BS, BS), jnp.float32),
        ],
        scratch_shapes=[pltpu.VMEM((BS, 2 * BS), jnp.float32)],
        cost_estimate=pl.CostEstimate(
            flops=60_000_000_000, bytes_accessed=200_000_000, transcendentals=0
        ),
        compiler_params=params(),
    )(*operands)


def solve_kernel(blocks, ids_ref, rows_ref, low_ref, inv_ref, out_ref):
    step = pl.program_id(0)
    done = []
    for k in range(PANELS):
        total = rows_ref[k]
        for j in range(k):
            total = total - mul_nt(done[j], split(low_ref[j, k * BS : (k + 1) * BS, :]))
        solved = mul_nt(split(total), split(inv_ref[k]))
        parts = []
        for b in range(blocks):
            live = ids_ref[step * blocks + b] > k
            parts.append(jnp.where(live, solved[b * BS : (b + 1) * BS], 0.0))
        solved = jnp.concatenate(parts, axis=0) if blocks > 1 else parts[0]
        out_ref[k] = solved
        done.append(split(solved))


def solve_rows(ids, rows, low, inv, blocks):
    count = rows.shape[1] // (blocks * BS)
    return pl.pallas_call(
        functools.partial(solve_kernel, blocks),
        grid=(count,),
        in_specs=[
            smem(),
            pl.BlockSpec((PANELS, blocks * BS, BS), lambda i: (0, i, 0)),
            vmem(),
            vmem(),
        ],
        out_specs=pl.BlockSpec((PANELS, blocks * BS, BS), lambda i: (0, i, 0)),
        out_shape=jax.ShapeDtypeStruct((PANELS, rows.shape[1], BS), jnp.float32),
        compiler_params=params(),
    )(ids, rows, low, inv)


def trail_kernel(
    head, local_cols, info_ref, front_ref, shift_ref, stay_ref, come0_ref, come1_ref,
    lead_ref, rest_ref, across_ref, factor_ref, out_ref, high_ref, low_ref,
):
    p = pl.program_id(0)

    @pl.when(p == 0)
    def _():
        for k in range(PANELS):
            high, low = split(across_ref[k])
            high_ref[k] = high
            low_ref[k] = low

    in_head = p < head
    total = jnp.zeros((BS, local_cols * BS), jnp.float32)
    for k in range(PANELS):
        left = split(jnp.where(in_head, lead_ref[k], rest_ref[k]))
        total = total + mul_nt(left, (high_ref[k], low_ref[k]))
    rows = lax.broadcasted_iota(jnp.int32, (BS, BS), 0)
    cols = lax.broadcasted_iota(jnp.int32, (BS, BS), 1)
    row_id = info_ref[4, p]
    panel = info_ref[8, 0]
    stays = info_ref[2, p] > 0
    comes = info_ref[3, p] > 0
    for s in range(local_cols):
        at = slice(s * BS, (s + 1) * BS)
        on_diag = (rows == cols) & (row_id == info_ref[5, s])
        block = front_ref[:, at] + jnp.where(on_diag, shift_ref[...], 0.0)
        for u, come_ref in enumerate((come0_ref, come1_ref)):
            piece = stay_ref[:, u * BS : (u + 1) * BS]
            block += jnp.where(stays & (info_ref[6, u] == s), piece, 0.0)
            block += jnp.where(comes & (info_ref[7, u] == s), come_ref[0], 0.0)
        block = block - total[:, at]
        if s == 0:
            own = jnp.where(in_head, lead_ref[panel], rest_ref[panel])
            in_panel = info_ref[9, 0] > 0
            block = jnp.where(in_panel & (row_id > panel), own, block)
            block = jnp.where(in_panel & (row_id == panel), factor_ref[...], block)
        out_ref[:, at] = block


def trail(info, front, shift, child, come0, come1, lead, rest, across, factor):
    local_rows = front.shape[0] // BS
    local_cols = front.shape[1] // BS
    head = lead.shape[1] // BS
    grid_spec = pltpu.PrefetchScalarGridSpec(
        num_scalar_prefetch=1,
        grid=(local_rows,),
        in_specs=[
            pl.BlockSpec((BS, local_cols * BS), lambda p, s: (p, 0)),
            pl.BlockSpec((1, BS), lambda p, s: (0, s[4, p])),
            pl.BlockSpec((BS, child.shape[1]), lambda p, s: (s[0, p], 0)),
            pl.BlockSpec((1, BS, BS), lambda p, s: (s[1, p], 0, 0)),
            pl.BlockSpec((1, BS, BS), lambda p, s: (s[1, p], 0, 0)),
            pl.BlockSpec((PANELS, BS, BS), lambda p, s: (0, jnp.minimum(p, head - 1), 0)),
            pl.BlockSpec((PANELS, BS, BS), lambda p, s: (0, jnp.maximum(p - head, 0), 0)),
            pl.BlockSpec(across.shape, lambda p, s: (0, 0, 0)),
            pl.BlockSpec((BS, BS), lambda p, s: (0, 0)),
        ],
        out_specs=pl.BlockSpec((BS, local_cols * BS), lambda p, s: (p, 0)),
        scratch_shapes=[pltpu.VMEM(across.shape, jnp.bfloat16)] * 2,
    )
    return pl.pallas_call(
        functools.partial(trail_kernel, head, local_cols),
        grid_spec=grid_spec,
        out_shape=jax.ShapeDtypeStruct(front.shape, jnp.float32),
        compiler_params=params(),
    )(info, front, shift, child, come0, come1, lead, rest, across, factor)


def on_device(front_orig, pivot_shift, child_update, child_map):
    n_row = lax.axis_size("row")
    n_col = lax.axis_size("col")
    row_id = lax.axis_index("row")
    col_id = lax.axis_index("col")
    half_rows = n_row // 2
    local_rows = front_orig.shape[0] // BS
    local_cols = front_orig.shape[1] // BS
    pair_count = child_update.shape[0] // BS // 2
    child_cols = child_update.shape[1] // BS
    stride = n_col // n_row
    head = stride
    side = row_id // half_rows

    paired = child_update.reshape(pair_count, 2, BS, child_cols, BS)
    swap = [(i, i ^ half_rows) for i in range(n_row)]
    come = [
        lax.ppermute(
            lax.dynamic_index_in_dim(paired[:, :, :, u], 1 - side, axis=1, keepdims=False),
            "row",
            swap,
        )
        for u in range(child_cols)
    ]

    mine_map = child_map[side]
    other_map = child_map[1 - side]
    slots = jnp.arange(local_rows, dtype=jnp.int32)

    def rows_of(table):
        wanted = table.reshape(pair_count, n_row)
        wanted = lax.dynamic_index_in_dim(wanted, row_id, axis=1, keepdims=False) // n_row
        hit = wanted[None, :] == slots[:, None]
        q = jnp.sum(jnp.where(hit, jnp.arange(pair_count, dtype=jnp.int32)[None, :], 0), axis=1)
        return q, jnp.any(hit, axis=1).astype(jnp.int32)

    def cols_of(table):
        wanted = table.reshape(child_cols, n_col)
        return lax.dynamic_index_in_dim(wanted, col_id, axis=1, keepdims=False) // n_col

    def line(values):
        values = jnp.atleast_1d(values).astype(jnp.int32)
        return jnp.pad(values, (0, 8 - values.shape[0]))

    stay_q, stays = rows_of(mine_map)
    come_q, comes = rows_of(other_map)
    row_blocks = slots * n_row + row_id
    col_blocks = jnp.arange(local_cols, dtype=jnp.int32) * n_col + col_id
    info = jnp.stack(
        [
            line(2 * stay_q + side),
            line(come_q),
            line(stays),
            line(comes),
            line(row_blocks),
            line(col_blocks),
            line(cols_of(mine_map)),
            line(cols_of(other_map)),
            line(jnp.minimum(col_id, PANELS - 1)),
            line(col_id < PANELS),
        ]
    )
    shift = pivot_shift.reshape(1, -1)
    column = panel_column(info, front_orig, shift, child_update, come[0])

    lead_rows = lax.all_gather(column[: head * BS], "col", axis=0)[:PANELS]

    lists = [
        [(i, j) for i in range(r, PANELS, n_row) for j in range(i + 1)] for r in range(n_row)
    ]
    length = max(len(blocks) for blocks in lists)
    length += length % 2
    width = length // 2
    where_block = {}
    table = []
    for r, blocks in enumerate(lists):
        entry = [j * head + (i // n_row) for i, j in blocks]
        table.append(entry + [0] * (length - len(entry)))
        for e, block in enumerate(blocks):
            where_block[block] = (r, e // width, e % width)
    table = jnp.array(table, jnp.int32).reshape(n_row, 2, width)
    parity = col_id % 2
    picks = table[row_id, parity]
    lead_tiles = lead_rows.reshape(PANELS * head, BS, BS)
    sent = jnp.stack(
        [lax.dynamic_index_in_dim(lead_tiles, picks[e], axis=0, keepdims=False) for e in range(width)]
    )
    mine = lax.all_gather(sent, "row", axis=0)
    other = lax.ppermute(mine, "col", [(i, i ^ 1) for i in range(n_col)])

    other, rest_part = lax.optimization_barrier((other, column[head * BS :]))
    rest_rows = lax.all_gather(rest_part, "col", axis=0)[:PANELS]
    low, inv, up = factor_group(
        functools.partial(lead_kernel, where_block),
        (parity.reshape(1), mine, other),
        [smem(), vmem(), vmem()],
    )
    inverses, factors = [inv], [up]

    pick = col_id // n_row
    source = col_id % n_row
    first = lax.dynamic_index_in_dim(
        lead_rows.reshape(PANELS, 1, head, BS, BS), pick, axis=2, keepdims=False
    )
    others = lax.dynamic_index_in_dim(
        rest_rows.reshape(PANELS, local_cols - 1, head, BS, BS), pick, axis=2, keepdims=False
    )
    across = jnp.concatenate([first, others], axis=1).reshape(PANELS, local_cols * BS, BS)
    across = jnp.where(row_id == source, across, 0.0)
    across, low = lax.optimization_barrier((across, low))
    bit = half_rows
    held = [0]
    begin = GROUP
    while bit:
        pairs = [
            (((c % n_row) ^ h) * n_col + c, ((c % n_row) ^ h ^ bit) * n_col + c)
            for c in range(n_col)
            for h in held
        ]
        came = lax.ppermute(across, ("row", "col"), pairs)
        if begin < PANELS:
            low, inv, up = factor_group(functools.partial(more_kernel, begin), (low,), [vmem()])
            inverses.append(inv)
            factors.append(up)
            begin += GROUP
            came, low = lax.optimization_barrier((came, low))
        across = across + came
        held = held + [h ^ bit for h in held]
        bit //= 2
    inv = jnp.concatenate(inverses, axis=0)
    up = jnp.concatenate(factors, axis=0)

    lead = solve_rows(row_blocks[:head], lead_rows, low, inv, head)
    rest = solve_rows(row_blocks[head:], rest_rows, low, inv, head)
    across = solve_rows(col_blocks, across, low, inv, local_cols)
    factor = lax.dynamic_index_in_dim(
        up, jnp.minimum(col_id, PANELS - 1), axis=0, keepdims=False
    ).T
    return trail(
        info, front_orig, shift, child_update, come[0], come[1], lead, rest, across, factor
    )


def solution(mesh):
    in_specs = (P("row", "col"), P(), P("row", "col"), P())
    out_specs = P("row", "col")
    return jax.shard_map(
        on_device, mesh=mesh, in_specs=in_specs, out_specs=out_specs, check_vma=False
    )
```
